256 devices in a mesh: ops: 16 (over z, core), sec: 16 (over y, x).
Axes of the slice: x: 4, y: 4, z: 8, core: 2. Of those that a mesh axis runs over, the one named last changes fastest.
Arguments:
- wavefunction: float32 [64, 256, 256], P('sec', 'ops'), may hold values from -64 to 64
- left_operators: float32 [64, 64, 256, 256], P('ops', 'sec'), may hold values from -8 to 8
- right_operators: float32 [64, 64, 256, 256], P('ops', 'sec'), may hold values from -8 to 8
- preconditioner: float32 [64, 256, 256], P('sec', 'ops'), may hold values from 1 to 10
- charges: int32 [64], P('ops'), may hold values from -1 to 1
- coupling: int32 [64, 64], P('ops', 'sec'), may hold values from 0 to 1
Outputs:
- correction: float32 [64, 256, 256], P('sec', 'ops')
- image_new: float32 [64, 256, 256], P('sec', 'ops')
The draws below stay inside these ranges and needn't reach their ends.
All inputs are finite; a program needn't handle non-finite values.
Results may differ from the reference program's by a relative error of at most 0.0007.
Values sent between devices are 32-bit elements; how exact they have to be, the bound alone decides.
No kernel may reach another device: no remote copies, remote signals or barrier semaphores. Data moves between devices by JAX's collectives and lax.ppermute only.
A program may use at most 64 MiB of HBM per device.

```python
import jax
import jax.numpy as jnp
from jax import lax

BLK = 256
TERMS = 64
PAIRS = 64


def with_diagonal(random_part, key, factor):
    diagonal = jax.random.uniform(key, random_part.shape[:-1], jnp.float32, 0.5, 1.5)
    row_index = lax.broadcasted_iota(jnp.int32, random_part.shape, 2)
    column_index = lax.broadcasted_iota(jnp.int32, random_part.shape, 3)
    identity = (row_index == column_index).astype(jnp.float32)
    return factor * (random_part * BLK ** (-0.5) + identity * diagonal[..., None])


def draw_left_operators(key, part):
    key = jax.random.fold_in(key, 11)
    key_noise, key_diag, key_offset = jax.random.split(key, 3)
    offset = jax.random.uniform(key_offset, (TERMS, PAIRS, 1, 1), jnp.float32, 0.25, 0.75)
    random_part = jnp.clip(jax.random.normal(key_noise, (TERMS, PAIRS, BLK, BLK), jnp.float32), -6.0, 6.0)
    return with_diagonal(random_part + offset, key_diag, 1.0)


def draw_right_operators(key, part):
    key = jax.random.fold_in(key, 23)
    key_noise, key_diag = jax.random.split(key)
    random_part = jnp.clip(jax.random.normal(key_noise, (TERMS, PAIRS, BLK, BLK), jnp.float32), -6.0, 6.0)
    return with_diagonal(random_part, key_diag, (TERMS // 2) ** (-0.5))


def draw_wavefunction(key, part):
    key = jax.random.fold_in(key, 3)
    key_noise, key_rows, key_cols = jax.random.split(key, 3)
    row_scale = jnp.exp(jax.random.uniform(key_rows, (PAIRS, BLK, 1), jnp.float32, 0.0, 1.16))
    column_scale = jnp.exp(jax.random.uniform(key_cols, (PAIRS, 1, BLK), jnp.float32, 0.0, 1.16))
    values = jnp.clip(jax.random.normal(key_noise, (PAIRS, BLK, BLK), jnp.float32), -6.5, 5.5) + 0.5
    return values * row_scale * column_scale


def level_field(key, row_weight, column_weight, entry_weight):
    key_rows, key_cols, key_entry = jax.random.split(key, 3)
    row_levels = jax.random.uniform(key_rows, (1, 16, 1, 1), jnp.float32, 0.0, 1.0)
    row_levels = jnp.broadcast_to(row_levels, (PAIRS, 16, BLK // 16, BLK)).reshape(PAIRS, BLK, BLK)
    column_levels = jax.random.uniform(key_cols, (1, 1, BLK), jnp.float32, 0.0, 1.0)
    entry_levels = jax.random.uniform(key_entry, (PAIRS, BLK, BLK), jnp.float32, 0.0, 1.0)
    exponent = row_weight * row_levels + column_weight * column_levels + entry_weight * entry_levels
    return jnp.clip(jnp.exp(2.302585 * exponent), 1.0, 10.0)


def draw_preconditioner(key, part):
    key = jax.random.fold_in(key, 31)
    return level_field(key, 0.6, 0.25, 0.15)


def draw_coupling(key, part):
    key = jax.random.fold_in(key, 5)
    key_density, key_levels = jax.random.split(key)
    density = jax.random.randint(key_density, (1, PAIRS), 1, 9)
    levels = jax.random.randint(key_levels, (TERMS, PAIRS), 0, 8)
    return (levels < density).astype(jnp.int32)


def set_ends(values, stream_key, least, top_value):
    index_at = [jax.random.randint(jax.random.fold_in(stream_key, axis), (), 0, length) for axis, length in enumerate(values.shape)]
    longest = values.shape.index(max(values.shape))
    next_to = index_at[:longest] + [(index_at[longest] + 1) % values.shape[longest]] + index_at[longest + 1:]
    return values.at[tuple(index_at)].set(least).at[tuple(next_to)].set(top_value)


def setup_inputs(seed: int = 0) -> dict:
    seeds = jax.random.split(jax.random.key(seed), 7)
    return {
        "wavefunction": draw_wavefunction(jax.random.fold_in(seeds[6], 71), 0),
        "left_operators": draw_left_operators(jax.random.fold_in(seeds[6], 71), 0),
        "right_operators": draw_right_operators(jax.random.fold_in(seeds[6], 71), 0),
        "preconditioner": draw_preconditioner(jax.random.fold_in(seeds[6], 71), 0),
        "charges": set_ends(jax.random.randint(seeds[4], (TERMS,), -1, 2), jax.random.fold_in(seeds[4], 1), -1, 1).astype(jnp.int32),
        "coupling": draw_coupling(jax.random.fold_in(seeds[6], 71), 0),
    }


PRECISE = lax.Precision.HIGHEST
EPSILON = 1e-06

def apply_hamiltonian(vector, left_operators, right_operators, charges, coupling):

    def add_term(accumulated, inputs):
        left_block, right_block, term_charge, term_mask = inputs
        left_applied = jnp.einsum('pij,pjl->pil', left_block.astype(jnp.float32), vector.astype(jnp.float32), precision=PRECISE)
        contribution = jnp.einsum('pil,pml->pim', left_applied, right_block.astype(jnp.float32), precision=PRECISE)
        contribution = contribution * term_mask.astype(jnp.float32)[:, None, None]
        padded = jnp.pad(contribution, ((1, 1), (0, 0), (0, 0)))
        start_index = (1 - term_charge).astype(jnp.int32)
        shifted = lax.dynamic_slice_in_dim(padded, start_index, PAIRS, 0)
        return (accumulated + shifted, None)
    accumulated, _ = lax.scan(add_term, jnp.zeros(vector.shape, jnp.float32), (left_operators, right_operators, charges, coupling))
    return accumulated

def reference(wavefunction, left_operators, right_operators, preconditioner, charges, coupling):
    entries = PAIRS * BLK * BLK
    image_psi = apply_hamiltonian(wavefunction, left_operators, right_operators, charges, coupling)
    psi_norm = jnp.sum(wavefunction * wavefunction)
    correlation = jnp.sum(wavefunction * image_psi)
    rayleigh = correlation / psi_norm
    scaled = (image_psi - rayleigh * wavefunction) / preconditioner
    projection = jnp.sum(wavefunction * scaled)
    orthogonal = scaled - projection / psi_norm * wavefunction
    squares = jnp.sum(orthogonal * orthogonal)
    correction = orthogonal / jnp.sqrt(squares / entries + EPSILON)
    image_new = apply_hamiltonian(correction, left_operators, right_operators, charges, coupling)
    return (correction, image_new)
```

```python
import functools

import jax
import jax.numpy as jnp
from jax import lax
from jax.experimental import pallas as pl
from jax.experimental.pallas import tpu as pltpu
from jax.sharding import PartitionSpec as P

EPSILON = 1e-06
F32 = jnp.float32
BF16 = jnp.bfloat16
BLK = 256
ROWS = 16
NZ = 8
NT = (((1,), (1,)), ((), ()))
NN = (((1,), (0,)), ((), ()))


def split(x):
    high = x.astype(BF16)
    return high, (x - high.astype(F32)).astype(BF16)


def product(a, b, dims):
    (ah, al), (bh, bl) = split(a), b
    dot = functools.partial(lax.dot_general, dimension_numbers=dims, preferred_element_type=F32)
    return dot(ah, bh) + (dot(ah, bl) + dot(al, bh))


def items_kernel(first, stride, has_start, core, charges, coupling, left, right, own, other, *rest):
    if has_start:
        start, *rest = rest
    *outs, acc, vector_high, vector_low = rest
    step, term = pl.program_id(0), pl.program_id(1)
    pair = first + stride * step

    @pl.when((step == 0) & (term == 0))
    def _():
        if has_start:
            acc[1:5] = start[...]
        else:
            acc[...] = jnp.zeros_like(acc)

    @pl.when(term == 0)
    def _():
        rows = pl.ds(pl.multiple_of(pair * ROWS, ROWS), ROWS)
        for z in range(NZ):
            a, b = own[z, rows, :], other[z, rows, :]
            for half, block in enumerate((jnp.where(core[0] == 0, a, b), jnp.where(core[0] == 0, b, a))):
                place = slice((2 * z + half) * ROWS, (2 * z + half + 1) * ROWS)
                vector_high[place, :], vector_low[place, :] = split(block)

    @pl.when(coupling[term, pair] > 0)
    def _():
        applied = product(left[0, 0], (vector_high[...], vector_low[...]), NN)
        block = product(applied, split(right[0, 0]), NT)
        target = pair + 1 + charges[term]
        acc[target] += block

    @pl.when((step == pl.num_programs(0) - 1) & (term == pl.num_programs(1) - 1))
    def _():
        outs[0][...] = acc[1:5]
        if len(outs) > 1:
            outs[1][...] = acc[0]
            outs[2][...] = acc[5]


def items(first, stride, core, charges, coupling, left, right, own, other, start=None):
    block = pl.BlockSpec((1, 1, BLK, BLK), lambda i, k: (k, first + stride * i, 0, 0))
    smem = pl.BlockSpec(memory_space=pltpu.SMEM)
    vmem = pl.BlockSpec(memory_space=pltpu.VMEM)
    inner = jax.ShapeDtypeStruct((4, BLK, BLK), F32)
    edge = jax.ShapeDtypeStruct((BLK, BLK), F32)
    outs = (inner, edge, edge) if start is None else (inner,)
    extra = () if start is None else (start,)
    return pl.pallas_call(
        functools.partial(items_kernel, first, stride, start is not None),
        grid=(2, 4),
        in_specs=[smem, smem, smem, block, block, vmem, vmem] + [vmem] * len(extra),
        out_specs=[vmem] * len(outs),
        out_shape=outs,
        scratch_shapes=[
            pltpu.VMEM((6, BLK, BLK), F32),
            pltpu.VMEM((BLK, BLK), BF16),
            pltpu.VMEM((BLK, BLK), BF16),
        ],
        compiler_params=pltpu.CompilerParams(vmem_limit_bytes=32 * 1024 * 1024),
        cost_estimate=pl.CostEstimate(flops=8 * 6 * 2 * BLK**3, bytes_accessed=8 * 2**19, transcendentals=0),
    )(core, charges, coupling, left, right, own, other, *extra)


def arrange_kernel(core, edges, inner, low, high, own, other, mine, theirs):
    from_low = edges[0] > 0
    from_high = edges[1] > 0
    dots = jnp.zeros((8, BLK), F32)
    norms = jnp.zeros((8, BLK), F32)
    for pair in range(4):
        for z in range(NZ):
            pieces = []
            for half in range(2):
                rows = slice((2 * z + half) * ROWS, (2 * z + half + 1) * ROWS)
                piece = inner[pair, rows, :]
                if pair == 0:
                    piece = piece + jnp.where(from_low, low[rows, :], 0.0)
                if pair == 3:
                    piece = piece + jnp.where(from_high, high[rows, :], 0.0)
                pieces.append(piece)
            place = slice(pair * ROWS, (pair + 1) * ROWS)
            a = jnp.where(core[0] == 0, pieces[0], pieces[1])
            b = jnp.where(core[0] == 0, pieces[1], pieces[0])
            mine[z, place, :] = a
            theirs[z, place, :] = b
            va, vb = own[z, place, :], other[z, place, :]
            d = a * va + b * vb
            n = va * va + vb * vb
            dots += d[:8] + d[8:]
            norms += n[:8] + n[8:]
    row = lax.broadcasted_iota(jnp.int32, (8, BLK), 0)
    sums = jnp.where(row == 0, jnp.sum(dots), 0.0) + jnp.where(row == 1, jnp.sum(norms) * (1.0 / 16), 0.0)
    for z in range(NZ):
        mine[z, 64:72, :] = sums
        theirs[z, 64:72, :] = sums


def arrange(core, edges, inner, low, high, own, other):
    smem = pl.BlockSpec(memory_space=pltpu.SMEM)
    vmem = pl.BlockSpec(memory_space=pltpu.VMEM)
    half = jax.ShapeDtypeStruct((NZ, 72, BLK), F32)
    return pl.pallas_call(
        arrange_kernel,
        in_specs=[smem, smem] + [vmem] * 5,
        out_specs=[vmem, vmem],
        out_shape=(half, half),
        compiler_params=pltpu.CompilerParams(vmem_limit_bytes=32 * 1024 * 1024),
    )(core, edges, inner, low, high, own, other)


SWAP = [(i, i ^ 1) for i in range(16)]
SAME_CORE = [[2 * z + c for z in range(NZ)] for c in range(2)]
UP = [(i, (i + 1) % 16) for i in range(16)]
DOWN = [(i, (i - 1) % 16) for i in range(16)]


def exchange(parts):
    return lax.all_to_all(parts, "ops", 0, 0, axis_index_groups=SAME_CORE)


def gather(slab):
    own = exchange(jnp.broadcast_to(slab[None], (NZ, *slab.shape)))
    return own, lax.ppermute(own, "ops", SWAP)


def image(own, other, core, edges, left, right, charges, coupling):
    inner, low, high = items(0, 3, core, charges, coupling, left, right, own, other)
    from_high = lax.ppermute(low, "sec", DOWN)
    from_low = lax.ppermute(high, "sec", UP)
    inner = items(1, 1, core, charges, coupling, left, right, own, other, inner)[0]
    mine, theirs = arrange(core, edges, inner, from_low, from_high, own, other)
    return jnp.sum(exchange(mine + lax.ppermute(theirs, "ops", SWAP)), axis=0)


def sec_sum(values):
    row = jnp.pad(jnp.stack(values), (0, 128 - len(values)))[None]
    sums = jnp.sum(lax.all_to_all(jnp.broadcast_to(row[None], (16, 1, 128)), "sec", 0, 0), axis=(0, 1))
    return [sums[i] for i in range(len(values))]


def on_device(wavefunction, left_operators, right_operators, preconditioner, charges, coupling):
    entries = wavefunction.size * lax.axis_size("ops") * lax.axis_size("sec")
    position = lax.axis_index("sec")
    core = (lax.axis_index("ops") % 2).astype(jnp.int32)[None]
    edges = jnp.stack([position > 0, position < 15]).astype(jnp.int32)
    operators = (left_operators, right_operators, charges, coupling)
    slab = wavefunction.reshape(64, BLK)
    weights = preconditioner.reshape(64, BLK)

    own, other = gather(slab)
    summed = image(own, other, core, edges, *operators)
    image_psi = summed[:64]
    correlation, psi_norm = sec_sum([summed[64, 0], summed[65, 0]])
    scaled = (image_psi - correlation / psi_norm * slab) / weights

    sums = jnp.stack([jnp.sum(slab * scaled), jnp.sum(scaled * scaled)])
    sums = jnp.broadcast_to(jnp.pad(sums, (0, 6))[:, None], (8, BLK))
    own, other = gather(jnp.concatenate([scaled, sums]))
    totals = jnp.sum(own[:, 64:66, 0] + other[:, 64:66, 0], axis=0)
    projection, scaled_squares = sec_sum([totals[0], totals[1]])
    image_scaled = image(own, other, core, edges, *operators)[:64]

    along = projection / psi_norm
    squares = jnp.maximum(scaled_squares - along * projection, 0.0)
    size = jnp.sqrt(squares / entries + EPSILON)
    correction = (scaled - along * slab) / size
    image_new = (image_scaled - along * image_psi) / size
    return correction.reshape(wavefunction.shape), image_new.reshape(wavefunction.shape)


def solution(mesh):
    placed = (
        P("sec", "ops", None),
        P("ops", "sec", None, None),
        P("ops", "sec", None, None),
        P("sec", "ops", None),
        P("ops"),
        P("ops", "sec"),
    )
    return jax.shard_map(
        on_device,
        mesh=mesh,
        in_specs=placed,
        out_specs=(P("sec", "ops", None), P("sec", "ops", None)),
        check_vma=False,
    )
```

```python
import functools

import jax
import jax.numpy as jnp
from jax import lax
from jax.experimental import pallas as pl
from jax.experimental.pallas import tpu as pltpu
from jax.sharding import PartitionSpec as P

EPSILON = 1e-06
F32 = jnp.float32
BF16 = jnp.bfloat16
BLK = 256
ROWS = 16
CORE, POSITION, CHARGES, COUPLING = 0, 1, 2, 6
NZ = 8
NT = (((1,), (1,)), ((), ()))
NN = (((1,), (0,)), ((), ()))
SMEM = pl.BlockSpec(memory_space=pltpu.SMEM)
VMEM = pl.BlockSpec(memory_space=pltpu.VMEM)
PARAMS = pltpu.CompilerParams(vmem_limit_bytes=24 * 1024 * 1024)


def shape(*dims, dtype=F32):
    return jax.ShapeDtypeStruct(dims, dtype)


def split(x):
    high = x.astype(BF16)
    return high, (x - high.astype(F32)).astype(BF16)


def dot(a, b, dims):
    return lax.dot_general(a, b, dims, preferred_element_type=F32)


def items(pairs, scalars, parts, own, other, acc):
    for slot, pair in enumerate(pairs):
        rows = slice(pair * ROWS, (pair + 1) * ROWS)
        pieces = []
        for z in range(NZ):
            a, b = own[z, rows, :], other[z, rows, :]
            pieces += [jnp.where(scalars[CORE] == 0, a, b), jnp.where(scalars[CORE] == 0, b, a)]
        vh, vl = split(jnp.concatenate(pieces, axis=0))
        for term in range(4):
            lh, ll, rh, rl = parts(slot, pair, term)
            uh, ul = split(dot(lh, vh, NN) + dot(lh, vl, NN) + dot(ll, vh, NN))
            acc[pair + 1 + scalars[CHARGES + term]] += dot(uh, rh, NT) + dot(uh, rl, NT) + dot(ul, rh, NT)


def kept_parts(left, right):
    return lambda slot, pair, term: (left[0, term, slot], left[1, term, slot], right[0, term, slot], right[1, term, slot])


EDGES, INNER = (0, 3), (1, 2)


def copies_of(pairs, left, right, blocks, semaphores):
    return [
        pltpu.make_async_copy(operator.at[term, pair], blocks.at[side, term, slot], semaphores.at[side, term, slot])
        for slot, pair in enumerate(pairs)
        for term in range(4)
        for side, operator in enumerate((left, right))
    ]


def fresh_parts(scalars, blocks, left_parts, right_parts):
    def parts(slot, pair, term):
        active = (scalars[COUPLING + 4 * term + pair] > 0).astype(F32)
        lh, ll = split(blocks[0, term, slot] * active)
        rh, rl = split(blocks[1, term, slot])
        left_parts[0, term, slot], left_parts[1, term, slot] = lh, ll
        right_parts[0, term, slot], right_parts[1, term, slot] = rh, rl
        return lh, ll, rh, rl

    return parts


def edge_parts_kernel(scalars, left, right, left_parts, right_parts, blocks, semaphores):
    copies = copies_of(EDGES, left, right, blocks, semaphores)
    for copy in copies:
        copy.start()
    parts = fresh_parts(scalars, blocks, left_parts, right_parts)
    for i, (slot, term) in enumerate((slot, term) for slot in range(2) for term in range(4)):
        copies[2 * i].wait()
        copies[2 * i + 1].wait()
        parts(slot, EDGES[slot], term)


def edges_of(acc, scalars, kept, given):
    kept[...] = acc[5 * scalars[CORE]]
    given[...] = acc[5 - 5 * scalars[CORE]]


def first_edge_kernel(scalars, left, right, left_parts, right_parts, own, other, acc, kept, given, blocks, semaphores):
    copies = copies_of(INNER, left, right, blocks, semaphores)
    for copy in copies:
        copy.start()
    acc[...] = jnp.zeros_like(acc)
    items(EDGES, scalars, kept_parts(left_parts, right_parts), own, other, acc)
    edges_of(acc, scalars, kept, given)
    for copy in copies:
        copy.wait()


def first_inner_kernel(scalars, blocks, own, other, start, acc, left_parts, right_parts):
    del start
    items(INNER, scalars, fresh_parts(scalars, blocks, left_parts, right_parts), own, other, acc)


def edge_kernel(scalars, left_parts, right_parts, own, other, acc, kept, given, totals):
    acc[...] = jnp.zeros_like(acc)
    items(EDGES, scalars, kept_parts(left_parts, right_parts), own, other, acc)
    edges_of(acc, scalars, kept, given)
    total = own[0, 64:72, :] + other[0, 64:72, :]
    for z in range(1, NZ):
        total += own[z, 64:72, :] + other[z, 64:72, :]
    totals[...] = total


def inner_kernel(scalars, left_parts, right_parts, own, other, start, acc):
    del start
    items(INNER, scalars, kept_parts(left_parts, right_parts), own, other, acc)


ACC, BLOCK = shape(6, BLK, BLK), shape(BLK, BLK)
BLOCKS = (2, 4, 2, BLK, BLK)
STAGED, PARTS = shape(*BLOCKS), shape(*BLOCKS, dtype=BF16)
COPIES = pltpu.SemaphoreType.DMA((2, 4, 2))


def on_blocks(kernel, outs, scalars, hbm, vmem, scratch=(), alias=None, flops=8 * 6 * 2 * BLK**3):
    return pl.pallas_call(
        kernel,
        in_specs=[SMEM] + [pl.BlockSpec(memory_space=pltpu.HBM)] * len(hbm) + [VMEM] * len(vmem),
        out_specs=[VMEM] * len(outs),
        out_shape=outs,
        scratch_shapes=scratch,
        input_output_aliases=alias or {},
        compiler_params=PARAMS,
        cost_estimate=pl.CostEstimate(flops=flops, bytes_accessed=8 * 2**19, transcendentals=0),
    )(scalars, *hbm, *vmem)


def arrange_kernel(scalars, acc, edge, own, other, *rest):
    *carried, mine, theirs = rest
    from_low = (scalars[CORE] == 1) & (scalars[POSITION] > 0)
    from_high = (scalars[CORE] == 0) & (scalars[POSITION] < 15)
    dots = jnp.zeros((8, BLK), F32)
    norms = jnp.zeros((8, BLK), F32)
    for pair in range(4):
        for z in range(NZ):
            pieces = []
            for half in range(2):
                rows = slice((2 * z + half) * ROWS, (2 * z + half + 1) * ROWS)
                piece = acc[pair + 1, rows, :]
                if pair == 0:
                    piece = piece + jnp.where(from_low, edge[rows, :], 0.0)
                if pair == 3:
                    piece = piece + jnp.where(from_high, edge[rows, :], 0.0)
                pieces.append(piece)
            place = slice(pair * ROWS, (pair + 1) * ROWS)
            a = jnp.where(scalars[CORE] == 0, pieces[0], pieces[1])
            b = jnp.where(scalars[CORE] == 0, pieces[1], pieces[0])
            mine[z, place, :] = a
            theirs[z, place, :] = b
            if not carried:
                va, vb = own[z, place, :], other[z, place, :]
                d = a * va + b * vb
                n = va * va + vb * vb
                dots += d[:8] + d[8:]
                norms += n[:8] + n[8:]
    if carried:
        sums = carried[0][...]
    else:
        row = lax.broadcasted_iota(jnp.int32, (8, BLK), 0)
        sums = jnp.where(row == 0, jnp.sum(dots), 0.0) + jnp.where(row == 1, jnp.sum(norms) * (1.0 / 16), 0.0)
    for z in range(NZ):
        mine[z, 64:72, :] = sums
        theirs[z, 64:72, :] = sums


def arrange(scalars, acc, edge, own, other, *carried):
    return pl.pallas_call(
        arrange_kernel,
        in_specs=[SMEM] + [VMEM] * (4 + len(carried)),
        out_specs=[VMEM, VMEM],
        out_shape=[shape(NZ, 72, BLK)] * 2,
        compiler_params=PARAMS,
    )(scalars, acc, edge, own, other, *carried)


def added(parts):
    total = parts[0]
    for z in range(1, NZ):
        total += parts[z]
    return total


def image_kernel(parts, image, sums):
    total = added(parts)
    image[...] = total[:64]
    for i in range(16):
        sums[i] = total[64:72, :128]


def scaled_kernel(parts, image, vector, weights, scaled, norm, sent):
    sums = parts[0]
    for i in range(1, 16):
        sums += parts[i]
    rayleigh = sums[0:1, 0:1] / sums[1:2, 0:1]
    norm[...] = jnp.broadcast_to(sums[1:2, 0:1], (8, BLK))
    value = (image[...] - rayleigh * vector[...]) / weights[...]
    scaled[...] = value
    row = lax.broadcasted_iota(jnp.int32, (8, BLK), 0)
    along = jnp.where(row == 0, jnp.sum(vector[...] * value), 0.0)
    rows = along + jnp.where(row == 1, jnp.sum(value * value), 0.0)
    for z in range(NZ):
        sent[z, :64, :] = value
        sent[z, 64:72, :] = rows


def finish_kernel(entries, parts, image, vector, scaled, norm, correction, image_new):
    total = added(parts)
    projection, squares = total[64:65, 0:1], total[65:66, 0:1]
    along = projection / norm[0:1, 0:1]
    squares = jnp.maximum(squares - along * projection, 0.0)
    size = jnp.sqrt(squares / entries + EPSILON)
    correction[...] = (scaled[...] - along * vector[...]) / size
    image_new[...] = (total[:64] - along * image[...]) / size


def local(kernel, outs, *args):
    return pl.pallas_call(
        kernel, in_specs=[VMEM] * len(args), out_specs=[VMEM] * len(outs), out_shape=outs, compiler_params=PARAMS
    )(*args)


SWAP = [(i, i ^ 1) for i in range(16)]
SAME_CORE = [[2 * z + c for z in range(NZ)] for c in range(2)]
TO_EDGES = [(o * 16 + s, o * 16 + (s + 2 * (o % 2) - 1) % 16) for o in range(16) for s in range(16)]
DIAGONAL = [(o * 16 + (s + o) % 16, o * 16 + s) for o in range(16) for s in range(16)]


def exchange(parts):
    return lax.all_to_all(parts, "ops", 0, 0, axis_index_groups=SAME_CORE)


def on_device(wavefunction, left_operators, right_operators, preconditioner, charges, coupling):
    entries = wavefunction.size * lax.axis_size("ops") * lax.axis_size("sec")
    core, position = lax.axis_index("ops") % 2, lax.axis_index("sec")
    scalars = jnp.concatenate([jnp.stack([core, position]).astype(jnp.int32), charges, coupling.reshape(16)])
    slab = wavefunction.reshape(64, BLK)
    weights = preconditioner.reshape(64, BLK)
    slab, scalars = lax.optimization_barrier((slab, scalars))
    operators = [pltpu.with_memory_space_constraint(x, pltpu.HBM) for x in (left_operators, right_operators)]

    def combined(acc, edge, own, other, *carried):
        mine, theirs = arrange(scalars, acc, edge, own, other, *carried)
        return exchange(mine + lax.ppermute(theirs, "ops", SWAP))

    def to_neighbour(kept, given):
        return lax.ppermute(kept + lax.ppermute(given, "ops", SWAP), ("ops", "sec"), TO_EDGES)

    own = exchange(jnp.broadcast_to(slab[None], (NZ, 64, BLK)))
    other = lax.ppermute(own, "ops", SWAP)
    scratch = [pltpu.VMEM(BLOCKS, F32), COPIES]
    edge_parts = on_blocks(edge_parts_kernel, [PARTS] * 2, scalars, operators, [], scratch, flops=0)
    outs = [ACC, BLOCK, BLOCK, STAGED]
    vectors = [*edge_parts, own, other]
    acc, kept, given, staged = on_blocks(first_edge_kernel, outs, scalars, operators, vectors, [COPIES])
    edge = to_neighbour(kept, given)
    outs, vectors = [ACC, PARTS, PARTS], [staged, own, other, acc]
    acc, *inner_parts = on_blocks(first_inner_kernel, outs, scalars, [], vectors, alias={4: 0})
    parts = combined(acc, edge, own, other)

    image, sums = local(image_kernel, [shape(64, BLK), shape(16, 8, 128)], parts)
    sums = lax.all_to_all(sums, "sec", 0, 0)
    outs = [shape(64, BLK), shape(8, BLK), shape(NZ, 72, BLK)]
    scaled, norm, sent = local(scaled_kernel, outs, sums, image, slab, weights)

    own = exchange(sent)
    other = lax.ppermute(own, "ops", SWAP)
    outs = [ACC, BLOCK, BLOCK, shape(8, BLK)]
    acc, kept, given, totals = on_blocks(edge_kernel, outs, scalars, [], [*edge_parts, own, other])
    edge = to_neighbour(kept, given)
    totals = lax.ppermute(totals, ("ops", "sec"), DIAGONAL)
    (acc,) = on_blocks(inner_kernel, [ACC], scalars, [], [*inner_parts, own, other, acc], alias={5: 0})
    parts = combined(acc, edge, own, other, totals)
    finish = functools.partial(finish_kernel, float(entries))
    correction, image_new = local(finish, [shape(64, BLK)] * 2, parts, image, slab, scaled, norm)
    return correction.reshape(wavefunction.shape), image_new.reshape(wavefunction.shape)


def solution(mesh):
    placed = (
        P("sec", "ops", None),
        P("ops", "sec", None, None),
        P("ops", "sec", None, None),
        P("sec", "ops", None),
        P("ops"),
        P("ops", "sec"),
    )
    return jax.shard_map(
        on_device,
        mesh=mesh,
        in_specs=placed,
        out_specs=(P("sec", "ops", None), P("sec", "ops", None)),
        check_vma=False,
    )
```

```python
import functools

import jax
import jax.numpy as jnp
from jax import lax
from jax.experimental import pallas as pl
from jax.experimental.pallas import tpu as pltpu
from jax.sharding import PartitionSpec as P

EPSILON = 1e-06
F32 = jnp.float32
BF16 = jnp.bfloat16
BLK = 256
ROWS = 16
NZ = 8
NT = (((1,), (1,)), ((), ()))
NN = (((1,), (0,)), ((), ()))
SMEM = pl.BlockSpec(memory_space=pltpu.SMEM)
VMEM = pl.BlockSpec(memory_space=pltpu.VMEM)
PARAMS = pltpu.CompilerParams(vmem_limit_bytes=24 * 1024 * 1024)


def shape(*dims, dtype=F32):
    return jax.ShapeDtypeStruct(dims, dtype)


def split(x):
    high = x.astype(BF16)
    return high, (x - high.astype(F32)).astype(BF16)


def dot(a, b, dims):
    return lax.dot_general(a, b, dims, preferred_element_type=F32)


def items(pairs, scalars, parts, own, other, acc):
    for slot, pair in enumerate(pairs):
        rows = slice(pair * ROWS, (pair + 1) * ROWS)
        pieces = []
        for z in range(NZ):
            a, b = own[z, rows, :], other[z, rows, :]
            pieces += [jnp.where(scalars[5, 0] == 0, a, b), jnp.where(scalars[5, 0] == 0, b, a)]
        vh, vl = split(jnp.concatenate(pieces, axis=0))
        for term in range(4):
            lh, ll, rh, rl = parts(slot, pair, term)
            uh, ul = split(dot(lh, vh, NN) + dot(lh, vl, NN) + dot(ll, vh, NN))
            acc[pair + 1 + scalars[4, term]] += dot(uh, rh, NT) + dot(uh, rl, NT) + dot(ul, rh, NT)


def kept_parts(left, right):
    return lambda slot, pair, term: (left[0, term, slot], left[1, term, slot], right[0, term, slot], right[1, term, slot])


EDGES, INNER = (0, 3), (1, 2)


def copies_of(pairs, left, right, blocks, semaphores):
    return [
        pltpu.make_async_copy(
            operator.at[term, pairs[slot]], blocks.at[side, term, slot], semaphores.at[side, term, slot]
        )
        for slot in range(2)
        for term in range(4)
        for side, operator in enumerate((left, right))
    ]


def fresh_parts(scalars, blocks, left_parts, right_parts):
    def parts(slot, pair, term):
        active = (scalars[term, pair] > 0).astype(F32)
        lh, ll = split(blocks[0, term, slot] * active)
        rh, rl = split(blocks[1, term, slot])
        left_parts[0, term, slot], left_parts[1, term, slot] = lh, ll
        right_parts[0, term, slot], right_parts[1, term, slot] = rh, rl
        return lh, ll, rh, rl

    return parts


def parts_kernel(pairs, scalars, left, right, *rest):
    *_, left_parts, right_parts, blocks, semaphores = rest
    copies = copies_of(pairs, left, right, blocks, semaphores)
    for copy in copies:
        copy.start()
    parts = fresh_parts(scalars, blocks, left_parts, right_parts)
    for i, (slot, term) in enumerate((slot, term) for slot in range(2) for term in range(4)):
        copies[2 * i].wait()
        copies[2 * i + 1].wait()
        parts(slot, pairs[slot], term)


def edges_of(acc, scalars, kept, given):
    kept[...] = acc[5 * scalars[5, 0]]
    given[...] = acc[5 - 5 * scalars[5, 0]]


def edge_kernel(scalars, left_parts, right_parts, own, other, acc, kept, given, *totals):
    acc[...] = jnp.zeros_like(acc)
    items(EDGES, scalars, kept_parts(left_parts, right_parts), own, other, acc)
    edges_of(acc, scalars, kept, given)
    if totals:
        totals[0][...] = added(own[:, 64:72, :]) + added(other[:, 64:72, :])


def inner_kernel(scalars, left_parts, right_parts, own, other, start, acc):
    del start
    items(INNER, scalars, kept_parts(left_parts, right_parts), own, other, acc)


ACC, BLOCK = shape(6, BLK, BLK), shape(BLK, BLK)
BLOCKS = (2, 4, 2, BLK, BLK)
PARTS = shape(*BLOCKS, dtype=BF16)
COPIES = pltpu.SemaphoreType.DMA((2, 4, 2))


def on_blocks(kernel, outs, scalars, hbm, vmem, scratch=(), alias=None, flops=8 * 6 * 2 * BLK**3):
    return pl.pallas_call(
        kernel,
        in_specs=[SMEM] + [pl.BlockSpec(memory_space=pltpu.HBM)] * len(hbm) + [VMEM] * len(vmem),
        out_specs=[VMEM] * len(outs),
        out_shape=outs,
        scratch_shapes=scratch,
        input_output_aliases=alias or {},
        compiler_params=PARAMS,
        cost_estimate=pl.CostEstimate(flops=flops, bytes_accessed=8 * 2**19, transcendentals=0),
    )(scalars, *hbm, *vmem)


def arrange_kernel(scalars, acc, edge, *rest):
    *vectors, mine, theirs = rest
    from_low = (scalars[5, 0] == 1) & (scalars[5, 1] > 0)
    from_high = (scalars[5, 0] == 0) & (scalars[5, 1] < 15)
    dots = jnp.zeros((8, BLK), F32)
    norms = jnp.zeros((8, BLK), F32)
    for pair in range(4):
        for z in range(NZ):
            pieces = []
            for half in range(2):
                rows = slice((2 * z + half) * ROWS, (2 * z + half + 1) * ROWS)
                piece = acc[pair + 1, rows, :]
                if pair == 0:
                    piece = piece + jnp.where(from_low, edge[rows, :], 0.0)
                if pair == 3:
                    piece = piece + jnp.where(from_high, edge[rows, :], 0.0)
                pieces.append(piece)
            place = slice(pair * ROWS, (pair + 1) * ROWS)
            a = jnp.where(scalars[5, 0] == 0, pieces[0], pieces[1])
            b = jnp.where(scalars[5, 0] == 0, pieces[1], pieces[0])
            mine[z, place, :] = a
            theirs[z, place, :] = b
            if vectors:
                va, vb = vectors[0][z, place, :], vectors[1][z, place, :]
                d = a * va + b * vb
                n = va * va + vb * vb
                dots += d[:8] + d[8:]
                norms += n[:8] + n[8:]
    if vectors:
        row = lax.broadcasted_iota(jnp.int32, (8, BLK), 0)
        sums = jnp.where(row == 0, jnp.sum(dots), 0.0) + jnp.where(row == 1, jnp.sum(norms) * (1.0 / 16), 0.0)
        for z in range(NZ):
            mine[z, 64:72, :] = sums
            theirs[z, 64:72, :] = sums


def arrange(scalars, acc, edge, *vectors):
    return pl.pallas_call(
        arrange_kernel,
        in_specs=[SMEM] + [VMEM] * (2 + len(vectors)),
        out_specs=[VMEM, VMEM],
        out_shape=[shape(NZ, 72 if vectors else 64, BLK)] * 2,
        compiler_params=PARAMS,
    )(scalars, acc, edge, *vectors)


def added(parts):
    total = parts[0]
    for z in range(1, NZ):
        total += parts[z]
    return total


def image_kernel(parts, vector, weights, image, sums):
    total = added(parts)
    correlation, norm = total[64:65, 0:1], total[65:66, 0:1]
    usable = norm > 1e-18
    near = jnp.where(usable, correlation, 0.0) / jnp.where(usable, norm, 1.0)
    image[...] = total[:64]
    rest = (total[:64] - near * vector[...]) / weights[...]
    weighted = vector[...] / weights[...]
    products = (vector[...] * rest, vector[...] * weighted, rest * rest, rest * weighted, weighted * weighted)
    values = [correlation, norm, *(jnp.sum(x, keepdims=True) for x in products), near]
    row = lax.broadcasted_iota(jnp.int32, (8, 128), 0)
    rows = jnp.zeros((8, 128), F32)
    for i, value in enumerate(values):
        rows = jnp.where(row == i, value, rows)
    for i in range(16):
        sums[i] = rows


def scaled_kernel(parts, image, vector, weights, scaled, norm, sent):
    columns = [parts[i] for i in range(16)]
    correlation = sum((x[0:1] for x in columns[1:]), columns[0][0:1])
    total = sum((x[1:2] for x in columns[1:]), columns[0][1:2])
    rayleigh = correlation / total
    along = jnp.zeros((1, 128), F32)
    squares = jnp.zeros((1, 128), F32)
    for x in columns:
        change = rayleigh - x[7:8]
        along += x[2:3] - change * x[3:4]
        squares += x[4:5] - change * (2.0 * x[5:6] - change * x[6:7])
    norm[...] = jnp.broadcast_to(total[:, 0:1], (8, BLK))
    value = (image[...] - rayleigh[:, 0:1] * vector[...]) / weights[...]
    scaled[...] = value
    row = lax.broadcasted_iota(jnp.int32, (8, BLK), 0)
    rows = jnp.where(row == 0, along[:, 0:1], squares[:, 0:1])
    for z in range(NZ):
        sent[z, :64, :] = value
        sent[z, 64:72, :] = rows


def finish_kernel(entries, parts, image, vector, scaled, norm, totals, correction, image_new):
    projection, squares = totals[0:1, 0:1], totals[1:2, 0:1]
    along = projection / norm[0:1, 0:1]
    squares = jnp.maximum(squares - along * projection, 0.0)
    size = jnp.sqrt(squares / entries + EPSILON)
    correction[...] = (scaled[...] - along * vector[...]) / size
    image_new[...] = (added(parts) - along * image[...]) / size


def local(kernel, outs, *args):
    return pl.pallas_call(
        kernel, in_specs=[VMEM] * len(args), out_specs=[VMEM] * len(outs), out_shape=outs, compiler_params=PARAMS
    )(*args)


SWAP = [(i, i ^ 1) for i in range(16)]
SAME_CORE = [[2 * z + c for z in range(NZ)] for c in range(2)]
TO_EDGES = [(o * 16 + s, o * 16 + (s + 2 * (o % 2) - 1) % 16) for o in range(16) for s in range(16)]


def exchange(parts):
    return lax.all_to_all(parts, "ops", 0, 0, axis_index_groups=SAME_CORE)


def on_device(wavefunction, left_operators, right_operators, preconditioner, charges, coupling):
    entries = wavefunction.size * lax.axis_size("ops") * lax.axis_size("sec")
    core, position = lax.axis_index("ops") % 2, lax.axis_index("sec")
    place = jnp.where(jnp.arange(4) == 0, core, position).astype(jnp.int32)
    scalars = jnp.concatenate([coupling, charges[None], place[None]])
    slab = wavefunction.reshape(64, BLK)
    weights = preconditioner.reshape(64, BLK)
    slab, scalars = lax.optimization_barrier((slab, scalars))
    operators = [pltpu.with_memory_space_constraint(x, pltpu.HBM) for x in (left_operators, right_operators)]

    def combined(acc, edge, *vectors):
        mine, theirs = arrange(scalars, acc, edge, *vectors)
        return exchange(mine + lax.ppermute(theirs, "ops", SWAP))

    def to_neighbour(kept, given):
        return lax.ppermute(kept + lax.ppermute(given, "ops", SWAP), ("ops", "sec"), TO_EDGES)

    own = exchange(jnp.broadcast_to(slab[None], (NZ, 64, BLK)))
    other = lax.ppermute(own, "ops", SWAP)
    scratch = [pltpu.VMEM(BLOCKS, F32), COPIES]
    split_edges, split_inner = (functools.partial(parts_kernel, pairs) for pairs in (EDGES, INNER))
    edge_parts = on_blocks(split_edges, [PARTS] * 2, scalars, operators, [], scratch, flops=0)
    acc, kept, given = on_blocks(edge_kernel, [ACC, BLOCK, BLOCK], scalars, [], [*edge_parts, own, other])
    edge = to_neighbour(kept, given)
    inner_parts = on_blocks(split_inner, [PARTS] * 2, scalars, operators, [], scratch, flops=0)
    (acc,) = on_blocks(inner_kernel, [ACC], scalars, [], [*inner_parts, own, other, acc], alias={5: 0})
    parts = combined(acc, edge, own, other)

    image, sums = local(image_kernel, [shape(64, BLK), shape(16, 8, 128)], parts, slab, weights)
    sums = lax.all_to_all(sums, "sec", 0, 0)
    outs = [shape(64, BLK), shape(8, BLK), shape(NZ, 72, BLK)]
    scaled, norm, sent = local(scaled_kernel, outs, sums, image, slab, weights)

    own = exchange(sent)
    other = lax.ppermute(own, "ops", SWAP)
    outs = [ACC, BLOCK, BLOCK, shape(8, BLK)]
    acc, kept, given, totals = on_blocks(edge_kernel, outs, scalars, [], [*edge_parts, own, other])
    edge = to_neighbour(kept, given)
    (acc,) = on_blocks(inner_kernel, [ACC], scalars, [], [*inner_parts, own, other, acc], alias={5: 0})
    parts = combined(acc, edge)
    finish = functools.partial(finish_kernel, float(entries))
    correction, image_new = local(finish, [shape(64, BLK)] * 2, parts, image, slab, scaled, norm, totals)
    return correction.reshape(wavefunction.shape), image_new.reshape(wavefunction.shape)


def solution(mesh):
    placed = (
        P("sec", "ops", None),
        P("ops", "sec", None, None),
        P("ops", "sec", None, None),
        P("sec", "ops", None),
        P("ops"),
        P("ops", "sec"),
    )
    return jax.shard_map(
        on_device,
        mesh=mesh,
        in_specs=placed,
        out_specs=(P("sec", "ops", None), P("sec", "ops", None)),
        check_vma=False,
    )
```

```python
import functools

import jax
import jax.numpy as jnp
from jax import lax
from jax.experimental import pallas as pl
from jax.experimental.pallas import tpu as pltpu
from jax.sharding import PartitionSpec as P

EPSILON = 1e-06
F32 = jnp.float32
BF16 = jnp.bfloat16
BLK = 256
ROWS = 16
NZ = 8
NT = (((1,), (1,)), ((), ()))
NN = (((1,), (0,)), ((), ()))
SMEM = pl.BlockSpec(memory_space=pltpu.SMEM)
VMEM = pl.BlockSpec(memory_space=pltpu.VMEM)
PARAMS = pltpu.CompilerParams(vmem_limit_bytes=24 * 1024 * 1024)


def shape(*dims, dtype=F32):
    return jax.ShapeDtypeStruct(dims, dtype)


def split(x):
    high = x.astype(BF16)
    return high, (x - high.astype(F32)).astype(BF16)


def dot(a, b, dims):
    return lax.dot_general(a, b, dims, preferred_element_type=F32)


def items(pairs, scalars, parts, own, other, acc):
    for slot, pair in enumerate(pairs):
        rows = slice(pair * ROWS, (pair + 1) * ROWS)
        pieces = []
        for z in range(NZ):
            a, b = own[z, rows, :], other[z, rows, :]
            pieces += [jnp.where(scalars[5, 0] == 0, a, b), jnp.where(scalars[5, 0] == 0, b, a)]
        vh, vl = split(jnp.concatenate(pieces, axis=0))
        for term in range(4):
            lh, ll, rh, rl = parts(slot, pair, term)
            uh, ul = split(dot(lh, vh, NN) + dot(lh, vl, NN) + dot(ll, vh, NN))
            acc[pair + 1 + scalars[4, term]] += dot(uh, rh, NT) + dot(uh, rl, NT) + dot(ul, rh, NT)


def kept_parts(left, right):
    return lambda slot, pair, term: (left[0, term, slot], left[1, term, slot], right[0, term, slot], right[1, term, slot])


EDGES, INNER = (0, 3), (1, 2)


def copies_of(pairs, left, right, blocks, semaphores):
    return [
        pltpu.make_async_copy(
            operator.at[term, pairs[slot]], blocks.at[side, term, slot], semaphores.at[side, term, slot]
        )
        for slot in range(2)
        for term in range(4)
        for side, operator in enumerate((left, right))
    ]


def fresh_parts(scalars, blocks, left_parts, right_parts):
    def parts(slot, pair, term):
        active = (scalars[term, pair] > 0).astype(F32)
        lh, ll = split(blocks[0, term, slot] * active)
        rh, rl = split(blocks[1, term, slot])
        left_parts[0, term, slot], left_parts[1, term, slot] = lh, ll
        right_parts[0, term, slot], right_parts[1, term, slot] = rh, rl
        return lh, ll, rh, rl

    return parts


def parts_kernel(pairs, scalars, left, right, *rest):
    *_, left_parts, right_parts, blocks, semaphores = rest
    copies = copies_of(pairs, left, right, blocks, semaphores)
    for copy in copies:
        copy.start()
    parts = fresh_parts(scalars, blocks, left_parts, right_parts)
    for i, (slot, term) in enumerate((slot, term) for slot in range(2) for term in range(4)):
        copies[2 * i].wait()
        copies[2 * i + 1].wait()
        parts(slot, pairs[slot], term)


def edges_of(acc, scalars, kept, given):
    kept[...] = acc[5 * scalars[5, 0]]
    given[...] = acc[5 - 5 * scalars[5, 0]]


def edge_kernel(scalars, left_parts, right_parts, own, other, acc, kept, given):
    acc[...] = jnp.zeros_like(acc)
    items(EDGES, scalars, kept_parts(left_parts, right_parts), own, other, acc)
    edges_of(acc, scalars, kept, given)


def rows_of(z, half):
    return pl.ds(pl.multiple_of((2 * z + half) * ROWS, ROWS), ROWS)


def last_edge_kernel(scalars, left_parts, right_parts, own, other, acc, low, high, given, totals):
    acc[...] = jnp.zeros_like(acc)
    items(EDGES, scalars, kept_parts(left_parts, right_parts), own, other, acc)
    core = scalars[5, 0]
    for z in range(NZ):
        low[z] = acc[0, rows_of(z, core), :]
        high[z] = acc[5, rows_of(z, core), :]
        given[0, z] = acc[0, rows_of(z, 1 - core), :]
        given[1, z] = acc[5, rows_of(z, 1 - core), :]
    totals[...] = added(own[:, 64:72, :]) + added(other[:, 64:72, :])


def inner_kernel(scalars, left_parts, right_parts, own, other, start, acc):
    del start
    items(INNER, scalars, kept_parts(left_parts, right_parts), own, other, acc)


def last_inner_kernel(scalars, left_parts, right_parts, own, other, start, acc, mine, theirs):
    del start
    items(INNER, scalars, kept_parts(left_parts, right_parts), own, other, acc)
    core = scalars[5, 0]
    for z in range(NZ):
        for pair in range(4):
            place = slice(pair * ROWS, (pair + 1) * ROWS)
            mine[z, place, :] = acc[pair + 1, rows_of(z, core), :]
            theirs[z, place, :] = acc[pair + 1, rows_of(z, 1 - core), :]


def last_sums_kernel(scalars, mine, theirs, from_low, from_high, sent):
    low, high = scalars[5, 1] > 0, scalars[5, 1] < 15
    sent[:, :16, :] = mine[:, :16, :] + theirs[:, :16, :] + jnp.where(low, from_low[...], 0.0)
    sent[:, 16:48, :] = mine[:, 16:48, :] + theirs[:, 16:48, :]
    sent[:, 48:, :] = mine[:, 48:, :] + theirs[:, 48:, :] + jnp.where(high, from_high[...], 0.0)


ACC, BLOCK = shape(6, BLK, BLK), shape(BLK, BLK)
BLOCKS = (2, 4, 2, BLK, BLK)
PARTS = shape(*BLOCKS, dtype=BF16)
COPIES = pltpu.SemaphoreType.DMA((2, 4, 2))


def on_blocks(kernel, outs, scalars, hbm, vmem, scratch=(), alias=None, flops=8 * 6 * 2 * BLK**3):
    return pl.pallas_call(
        kernel,
        in_specs=[SMEM] + [pl.BlockSpec(memory_space=pltpu.HBM)] * len(hbm) + [VMEM] * len(vmem),
        out_specs=[VMEM] * len(outs),
        out_shape=outs,
        scratch_shapes=scratch,
        input_output_aliases=alias or {},
        compiler_params=PARAMS,
        cost_estimate=pl.CostEstimate(flops=flops, bytes_accessed=8 * 2**19, transcendentals=0),
    )(scalars, *hbm, *vmem)


def arrange_kernel(scalars, acc, edge, own, other, mine, theirs):
    from_low = (scalars[5, 0] == 1) & (scalars[5, 1] > 0)
    from_high = (scalars[5, 0] == 0) & (scalars[5, 1] < 15)
    dots = jnp.zeros((8, BLK), F32)
    norms = jnp.zeros((8, BLK), F32)
    for pair in range(4):
        for z in range(NZ):
            pieces = []
            for half in range(2):
                rows = slice((2 * z + half) * ROWS, (2 * z + half + 1) * ROWS)
                piece = acc[pair + 1, rows, :]
                if pair == 0:
                    piece = piece + jnp.where(from_low, edge[rows, :], 0.0)
                if pair == 3:
                    piece = piece + jnp.where(from_high, edge[rows, :], 0.0)
                pieces.append(piece)
            place = slice(pair * ROWS, (pair + 1) * ROWS)
            a = jnp.where(scalars[5, 0] == 0, pieces[0], pieces[1])
            b = jnp.where(scalars[5, 0] == 0, pieces[1], pieces[0])
            mine[z, place, :] = a
            theirs[z, place, :] = b
            va, vb = own[z, place, :], other[z, place, :]
            d = a * va + b * vb
            n = va * va + vb * vb
            dots += d[:8] + d[8:]
            norms += n[:8] + n[8:]
    row = lax.broadcasted_iota(jnp.int32, (8, BLK), 0)
    sums = jnp.where(row == 0, jnp.sum(dots), 0.0) + jnp.where(row == 1, jnp.sum(norms) * (1.0 / 16), 0.0)
    for z in range(NZ):
        mine[z, 64:72, :] = sums
        theirs[z, 64:72, :] = sums


def added(parts):
    total = parts[0]
    for z in range(1, NZ):
        total += parts[z]
    return total


def image_kernel(parts, vector, weights, image, sums):
    total = added(parts)
    correlation, norm = total[64:65, 0:1], total[65:66, 0:1]
    usable = norm > 1e-18
    near = jnp.where(usable, correlation, 0.0) / jnp.where(usable, norm, 1.0)
    image[...] = total[:64]
    rest = (total[:64] - near * vector[...]) / weights[...]
    weighted = vector[...] / weights[...]
    products = (vector[...] * rest, vector[...] * weighted, rest * rest, rest * weighted, weighted * weighted)
    values = [correlation, norm, *(jnp.sum(x, keepdims=True) for x in products), near]
    row = lax.broadcasted_iota(jnp.int32, (8, 128), 0)
    rows = jnp.zeros((8, 128), F32)
    for i, value in enumerate(values):
        rows = jnp.where(row == i, value, rows)
    for i in range(16):
        sums[i] = rows


def scaled_kernel(parts, image, vector, weights, scaled, norm, sent):
    columns = [parts[i] for i in range(16)]
    correlation = sum((x[0:1] for x in columns[1:]), columns[0][0:1])
    total = sum((x[1:2] for x in columns[1:]), columns[0][1:2])
    rayleigh = correlation / total
    along = jnp.zeros((1, 128), F32)
    squares = jnp.zeros((1, 128), F32)
    for x in columns:
        change = rayleigh - x[7:8]
        along += x[2:3] - change * x[3:4]
        squares += x[4:5] - change * (2.0 * x[5:6] - change * x[6:7])
    norm[...] = jnp.broadcast_to(total[:, 0:1], (8, BLK))
    value = (image[...] - rayleigh[:, 0:1] * vector[...]) / weights[...]
    scaled[...] = value
    row = lax.broadcasted_iota(jnp.int32, (8, BLK), 0)
    rows = jnp.where(row == 0, along[:, 0:1], squares[:, 0:1])
    for z in range(NZ):
        sent[z, :64, :] = value
        sent[z, 64:72, :] = rows


def finish_kernel(entries, parts, image, vector, scaled, norm, totals, correction, image_new):
    projection, squares = totals[0:1, 0:1], totals[1:2, 0:1]
    along = projection / norm[0:1, 0:1]
    squares = jnp.maximum(squares - along * projection, 0.0)
    size = jnp.sqrt(squares / entries + EPSILON)
    correction[...] = (scaled[...] - along * vector[...]) / size
    image_new[...] = (added(parts) - along * image[...]) / size


def local(kernel, outs, *args):
    return pl.pallas_call(
        kernel, in_specs=[VMEM] * len(args), out_specs=[VMEM] * len(outs), out_shape=outs, compiler_params=PARAMS
    )(*args)


UP = [(i, (i + 1) % 16) for i in range(16)]
DOWN = [(i, (i - 1) % 16) for i in range(16)]
SWAP = [(i, i ^ 1) for i in range(16)]
SAME_CORE = [[2 * z + c for z in range(NZ)] for c in range(2)]
TO_EDGES = [(o * 16 + s, o * 16 + (s + 2 * (o % 2) - 1) % 16) for o in range(16) for s in range(16)]


def exchange(parts):
    return lax.all_to_all(parts, "ops", 0, 0, axis_index_groups=SAME_CORE)


def on_device(wavefunction, left_operators, right_operators, preconditioner, charges, coupling):
    entries = wavefunction.size * lax.axis_size("ops") * lax.axis_size("sec")
    core, position = lax.axis_index("ops") % 2, lax.axis_index("sec")
    place = jnp.where(jnp.arange(4) == 0, core, position).astype(jnp.int32)
    scalars = jnp.concatenate([coupling, charges[None], place[None]])
    slab = wavefunction.reshape(64, BLK)
    weights = preconditioner.reshape(64, BLK)
    slab, scalars = lax.optimization_barrier((slab, scalars))
    operators = [pltpu.with_memory_space_constraint(x, pltpu.HBM) for x in (left_operators, right_operators)]

    def swap(x):
        return lax.ppermute(x, "ops", SWAP)

    own = exchange(jnp.broadcast_to(slab[None], (NZ, 64, BLK)))
    other = swap(own)
    scratch = [pltpu.VMEM(BLOCKS, F32), COPIES]
    split_edges, split_inner = (functools.partial(parts_kernel, pairs) for pairs in (EDGES, INNER))
    edge_parts = on_blocks(split_edges, [PARTS] * 2, scalars, operators, [], scratch, flops=0)
    acc, kept, given = on_blocks(edge_kernel, [ACC, BLOCK, BLOCK], scalars, [], [*edge_parts, own, other])
    edge = lax.ppermute(kept + swap(given), ("ops", "sec"), TO_EDGES)
    inner_parts = on_blocks(split_inner, [PARTS] * 2, scalars, operators, [], scratch, flops=0)
    (acc,) = on_blocks(inner_kernel, [ACC], scalars, [], [*inner_parts, own, other, acc], alias={5: 0})
    halves, vectors = [shape(NZ, 72, BLK)] * 2, [acc, edge, own, other]
    mine, theirs = on_blocks(arrange_kernel, halves, scalars, [], vectors, flops=0)
    parts = exchange(mine + swap(theirs))

    image, sums = local(image_kernel, [shape(64, BLK), shape(16, 8, 128)], parts, slab, weights)
    sums = lax.all_to_all(sums, "sec", 0, 0)
    outs = [shape(64, BLK), shape(8, BLK), shape(NZ, 72, BLK)]
    scaled, norm, sent = local(scaled_kernel, outs, sums, image, slab, weights)

    own = exchange(sent)
    other = swap(own)
    strip = shape(NZ, ROWS, BLK)
    outs = [ACC, strip, strip, shape(2, NZ, ROWS, BLK), shape(8, BLK)]
    acc, low, high, given, totals = on_blocks(last_edge_kernel, outs, scalars, [], [*edge_parts, own, other])
    given = swap(given)
    from_high = lax.ppermute(low + given[0], "sec", DOWN)
    from_low = lax.ppermute(high + given[1], "sec", UP)
    outs, vectors = [ACC, *[shape(NZ, 64, BLK)] * 2], [*inner_parts, own, other, acc]
    _, mine, theirs = on_blocks(last_inner_kernel, outs, scalars, [], vectors, alias={5: 0})
    vectors = [mine, swap(theirs), from_low, from_high]
    (sent,) = on_blocks(last_sums_kernel, [shape(NZ, 64, BLK)], scalars, [], vectors, flops=0)
    parts = exchange(sent)
    finish = functools.partial(finish_kernel, float(entries))
    correction, image_new = local(finish, [shape(64, BLK)] * 2, parts, image, slab, scaled, norm, totals)
    return correction.reshape(wavefunction.shape), image_new.reshape(wavefunction.shape)


def solution(mesh):
    placed = (
        P("sec", "ops", None),
        P("ops", "sec", None, None),
        P("ops", "sec", None, None),
        P("sec", "ops", None),
        P("ops"),
        P("ops", "sec"),
    )
    return jax.shard_map(
        on_device,
        mesh=mesh,
        in_specs=placed,
        out_specs=(P("sec", "ops", None), P("sec", "ops", None)),
        check_vma=False,
    )
```

```python
import functools

import jax
import jax.numpy as jnp
from jax import lax
from jax.experimental import pallas as pl
from jax.experimental.pallas import tpu as pltpu
from jax.sharding import PartitionSpec as P

EPSILON = 1e-06
F32 = jnp.float32
BF16 = jnp.bfloat16
BLK = 256
HALF = 128
ROWS = 16
NZ = 8
NT = (((1,), (1,)), ((), ()))
NN = (((1,), (0,)), ((), ()))
SMEM = pl.BlockSpec(memory_space=pltpu.SMEM)
VMEM = pl.BlockSpec(memory_space=pltpu.VMEM)
PARAMS = pltpu.CompilerParams(vmem_limit_bytes=24 * 1024 * 1024)


def shape(*dims, dtype=F32):
    return jax.ShapeDtypeStruct(dims, dtype)


def split(x):
    high = x.astype(BF16)
    return high, (x - high.astype(F32)).astype(BF16)


def dot(a, b, dims):
    return lax.dot_general(a, b, dims, preferred_element_type=F32)


def rows_at(x, z, pair):
    rows = slice(pair * ROWS, (pair + 1) * ROWS)
    if x.shape[2] == BLK:
        return x[z, rows, :]
    return jnp.concatenate([x[z, rows, :], x[z, 64 + pair * ROWS : 64 + (pair + 1) * ROWS, :]], axis=1)


def put_rows(x, z, rows, value):
    x[z, rows, :] = value[:, :HALF]
    x[z, 64 + rows.start : 64 + rows.stop, :] = value[:, HALF:]


def items(pairs, scalars, parts, own, other, acc):
    for slot, pair in enumerate(pairs):
        pieces = []
        for z in range(NZ):
            a, b = rows_at(own, z, pair), rows_at(other, z, pair)
            pieces += [jnp.where(scalars[5, 0] == 0, a, b), jnp.where(scalars[5, 0] == 0, b, a)]
        vh, vl = split(jnp.concatenate(pieces, axis=0))
        for term in range(4):
            lh, ll, rh, rl = parts(slot, pair, term)
            uh, ul = split(dot(lh, vh, NN) + dot(lh, vl, NN) + dot(ll, vh, NN))
            acc[pair + 1 + scalars[4, term]] += dot(uh, rh, NT) + dot(uh, rl, NT) + dot(ul, rh, NT)


def kept_parts(left, right):
    return lambda slot, pair, term: (left[0, term, slot], left[1, term, slot], right[0, term, slot], right[1, term, slot])


EDGES, INNER = (0, 3), (1, 2)


def copies_of(pairs, left, right, blocks, semaphores):
    return [
        pltpu.make_async_copy(
            operator.at[term, pairs[slot]], blocks.at[side, term, slot], semaphores.at[side, term, slot]
        )
        for slot in range(2)
        for term in range(4)
        for side, operator in enumerate((left, right))
    ]


def fresh_parts(scalars, blocks, left_parts, right_parts):
    def parts(slot, pair, term):
        active = (scalars[term, pair] > 0).astype(F32)
        lh, ll = split(blocks[0, term, slot] * active)
        rh, rl = split(blocks[1, term, slot])
        left_parts[0, term, slot], left_parts[1, term, slot] = lh, ll
        right_parts[0, term, slot], right_parts[1, term, slot] = rh, rl
        return lh, ll, rh, rl

    return parts


def split_parts(pairs, scalars, copies, blocks, left_parts, right_parts):
    parts = fresh_parts(scalars, blocks, left_parts, right_parts)
    for i, (slot, term) in enumerate((slot, term) for slot in range(2) for term in range(4)):
        copies[2 * i].wait()
        copies[2 * i + 1].wait()
        parts(slot, pairs[slot], term)


def first_parts_kernel(left, right, coupling, charges, left_parts, right_parts, scalars, blocks, semaphores, ends):
    small = [
        pltpu.make_async_copy(coupling, scalars.at[pl.ds(0, 4), :], ends.at[0]),
        pltpu.make_async_copy(charges, scalars.at[4], ends.at[1]),
    ]
    copies = copies_of(EDGES, left, right, blocks, semaphores)
    for copy in small + copies:
        copy.start()
    for copy in small:
        copy.wait()
    scalars[5, 0] = lax.rem(lax.axis_index("ops"), 2)
    scalars[5, 1] = lax.axis_index("sec")
    scalars[5, 2] = 0
    scalars[5, 3] = 0
    split_parts(EDGES, scalars, copies, blocks, left_parts, right_parts)


def parts_kernel(scalars, left, right, left_parts, right_parts, blocks, semaphores):
    copies = copies_of(INNER, left, right, blocks, semaphores)
    for copy in copies:
        copy.start()
    split_parts(INNER, scalars, copies, blocks, left_parts, right_parts)


def edges_of(acc, scalars, kept, given):
    kept[...] = acc[5 * scalars[5, 0]]
    given[...] = acc[5 - 5 * scalars[5, 0]]


def edge_kernel(scalars, left_parts, right_parts, own, other, acc, kept, given):
    acc[...] = jnp.zeros_like(acc)
    items(EDGES, scalars, kept_parts(left_parts, right_parts), own, other, acc)
    edges_of(acc, scalars, kept, given)


def rows_of(z, half):
    return pl.ds(pl.multiple_of((2 * z + half) * ROWS, ROWS), ROWS)


def last_edge_kernel(scalars, left_parts, right_parts, own, other, acc, low, high, given, totals):
    acc[...] = jnp.zeros_like(acc)
    items(EDGES, scalars, kept_parts(left_parts, right_parts), own, other, acc)
    core = scalars[5, 0]
    for z in range(NZ):
        low[z] = acc[0, rows_of(z, core), :]
        high[z] = acc[5, rows_of(z, core), :]
        given[0, z] = acc[0, rows_of(z, 1 - core), :]
        given[1, z] = acc[5, rows_of(z, 1 - core), :]
    totals[...] = added(own[:, 128:136, :]) + added(other[:, 128:136, :])


def inner_kernel(scalars, left_parts, right_parts, own, other, start, acc):
    del start
    items(INNER, scalars, kept_parts(left_parts, right_parts), own, other, acc)


def last_inner_kernel(scalars, left_parts, right_parts, own, other, start, acc, mine, theirs):
    del start
    items(INNER, scalars, kept_parts(left_parts, right_parts), own, other, acc)
    core = scalars[5, 0]
    for z in range(NZ):
        for pair in range(4):
            place = slice(pair * ROWS, (pair + 1) * ROWS)
            mine[z, place, :] = acc[pair + 1, rows_of(z, core), :]
            theirs[z, place, :] = acc[pair + 1, rows_of(z, 1 - core), :]


def last_sums_kernel(scalars, mine, theirs, from_low, from_high, sent):
    low, high = scalars[5, 1] > 0, scalars[5, 1] < 15
    sent[:, :16, :] = mine[:, :16, :] + theirs[:, :16, :] + jnp.where(low, from_low[...], 0.0)
    sent[:, 16:48, :] = mine[:, 16:48, :] + theirs[:, 16:48, :]
    sent[:, 48:, :] = mine[:, 48:, :] + theirs[:, 48:, :] + jnp.where(high, from_high[...], 0.0)


ACC, BLOCK = shape(6, BLK, BLK), shape(BLK, BLK)
BLOCKS = (2, 4, 2, BLK, BLK)
PARTS = shape(*BLOCKS, dtype=BF16)
COPIES = pltpu.SemaphoreType.DMA((2, 4, 2))


def on_blocks(kernel, outs, scalars, hbm, vmem, scratch=(), alias=None, flops=8 * 6 * 2 * BLK**3):
    return pl.pallas_call(
        kernel,
        in_specs=[SMEM] + [pl.BlockSpec(memory_space=pltpu.HBM)] * len(hbm) + [VMEM] * len(vmem),
        out_specs=[VMEM] * len(outs),
        out_shape=outs,
        scratch_shapes=scratch,
        input_output_aliases=alias or {},
        compiler_params=PARAMS,
        cost_estimate=pl.CostEstimate(flops=flops, bytes_accessed=8 * 2**19, transcendentals=0),
    )(scalars, *hbm, *vmem)


def arrange_kernel(scalars, acc, edge, own, other, mine, theirs):
    from_low = (scalars[5, 0] == 1) & (scalars[5, 1] > 0)
    from_high = (scalars[5, 0] == 0) & (scalars[5, 1] < 15)
    dots = jnp.zeros((8, BLK), F32)
    norms = jnp.zeros((8, BLK), F32)
    for pair in range(4):
        for z in range(NZ):
            pieces = []
            for half in range(2):
                rows = slice((2 * z + half) * ROWS, (2 * z + half + 1) * ROWS)
                piece = acc[pair + 1, rows, :]
                if pair == 0:
                    piece = piece + jnp.where(from_low, edge[rows, :], 0.0)
                if pair == 3:
                    piece = piece + jnp.where(from_high, edge[rows, :], 0.0)
                pieces.append(piece)
            place = slice(pair * ROWS, (pair + 1) * ROWS)
            a = jnp.where(scalars[5, 0] == 0, pieces[0], pieces[1])
            b = jnp.where(scalars[5, 0] == 0, pieces[1], pieces[0])
            put_rows(mine, z, place, a)
            put_rows(theirs, z, place, b)
            va, vb = own[z, place, :], other[z, place, :]
            d = a * va + b * vb
            n = va * va + vb * vb
            dots += d[:8] + d[8:]
            norms += n[:8] + n[8:]
    row = lax.broadcasted_iota(jnp.int32, (8, HALF), 0)
    sums = jnp.where(row == 0, jnp.sum(dots), 0.0) + jnp.where(row == 1, jnp.sum(norms) * (1.0 / 16), 0.0)
    for z in range(NZ):
        mine[z, 128:136, :] = sums
        theirs[z, 128:136, :] = sums


def added(parts):
    total = parts[0]
    for z in range(1, NZ):
        total += parts[z]
    return total


def image_kernel(parts, vector, weights, image, sums):
    total = added(parts)
    correlation, norm = total[128:129, 0:1], total[129:130, 0:1]
    summed = jnp.concatenate([total[:64], total[64:128]], axis=1)
    usable = norm > 1e-18
    near = jnp.where(usable, correlation, 0.0) / jnp.where(usable, norm, 1.0)
    image[...] = summed
    rest = (summed - near * vector[...]) / weights[...]
    weighted = vector[...] / weights[...]
    products = (vector[...] * rest, vector[...] * weighted, rest * rest, rest * weighted, weighted * weighted)
    values = [correlation, norm, *(jnp.sum(x, keepdims=True) for x in products), near]
    row = lax.broadcasted_iota(jnp.int32, (8, 128), 0)
    rows = jnp.zeros((8, 128), F32)
    for i, value in enumerate(values):
        rows = jnp.where(row == i, value, rows)
    for i in range(16):
        sums[i] = rows


def scaled_kernel(parts, image, vector, weights, scaled, norm, sent):
    columns = [parts[i] for i in range(16)]
    correlation = sum((x[0:1] for x in columns[1:]), columns[0][0:1])
    total = sum((x[1:2] for x in columns[1:]), columns[0][1:2])
    rayleigh = correlation / total
    along = jnp.zeros((1, 128), F32)
    squares = jnp.zeros((1, 128), F32)
    for x in columns:
        change = rayleigh - x[7:8]
        along += x[2:3] - change * x[3:4]
        squares += x[4:5] - change * (2.0 * x[5:6] - change * x[6:7])
    norm[...] = jnp.broadcast_to(total[:, 0:1], (8, BLK))
    value = (image[...] - rayleigh[:, 0:1] * vector[...]) / weights[...]
    scaled[...] = value
    row = lax.broadcasted_iota(jnp.int32, (8, HALF), 0)
    rows = jnp.where(row == 0, along[:, 0:1], squares[:, 0:1])
    for z in range(NZ):
        put_rows(sent, z, slice(0, 64), value)
        sent[z, 128:136, :] = rows


def finish_kernel(entries, parts, image, vector, scaled, norm, totals, correction, image_new):
    projection, squares = totals[0:1, 0:1], totals[1:2, 0:1]
    along = projection / norm[0:1, 0:1]
    squares = jnp.maximum(squares - along * projection, 0.0)
    size = jnp.sqrt(squares / entries + EPSILON)
    correction[...] = (scaled[...] - along * vector[...]) / size
    image_new[...] = (added(parts) - along * image[...]) / size


def local(kernel, outs, *args):
    return pl.pallas_call(
        kernel, in_specs=[VMEM] * len(args), out_specs=[VMEM] * len(outs), out_shape=outs, compiler_params=PARAMS
    )(*args)


UP = [(i, (i + 1) % 16) for i in range(16)]
DOWN = [(i, (i - 1) % 16) for i in range(16)]
SWAP = [(i, i ^ 1) for i in range(16)]
SAME_CORE = [[2 * z + c for z in range(NZ)] for c in range(2)]
TO_EDGES = [(o * 16 + s, o * 16 + (s + 2 * (o % 2) - 1) % 16) for o in range(16) for s in range(16)]


def exchange(parts):
    return lax.all_to_all(parts, "ops", 0, 0, axis_index_groups=SAME_CORE)


def on_device(wavefunction, left_operators, right_operators, preconditioner, charges, coupling):
    entries = wavefunction.size * lax.axis_size("ops") * lax.axis_size("sec")
    slab = wavefunction.reshape(64, BLK)
    weights = preconditioner.reshape(64, BLK)
    operators = [pltpu.with_memory_space_constraint(x, pltpu.HBM) for x in (left_operators, right_operators)]

    def swap(x):
        return lax.ppermute(x, "ops", SWAP)

    own = exchange(jnp.broadcast_to(slab[None], (NZ, 64, BLK)))
    other = swap(own)
    scratch = [pltpu.VMEM(BLOCKS, F32), COPIES]
    hbm = pl.BlockSpec(memory_space=pltpu.HBM)
    *edge_parts, scalars = pl.pallas_call(
        first_parts_kernel,
        in_specs=[hbm] * 4,
        out_specs=[VMEM, VMEM, SMEM],
        out_shape=[PARTS, PARTS, shape(6, 4, dtype=jnp.int32)],
        scratch_shapes=[*scratch, pltpu.SemaphoreType.DMA((2,))],
        compiler_params=PARAMS,
        cost_estimate=pl.CostEstimate(flops=0, bytes_accessed=8 * 2**19, transcendentals=0),
    )(*operators, *(pltpu.with_memory_space_constraint(x, pltpu.HBM) for x in (coupling, charges)))
    acc, kept, given = on_blocks(edge_kernel, [ACC, BLOCK, BLOCK], scalars, [], [*edge_parts, own, other])
    edge = lax.ppermute(kept + swap(given), ("ops", "sec"), TO_EDGES)
    inner_parts = on_blocks(parts_kernel, [PARTS] * 2, scalars, operators, [], scratch, flops=0)
    (acc,) = on_blocks(inner_kernel, [ACC], scalars, [], [*inner_parts, own, other, acc], alias={5: 0})
    halves, vectors = [shape(NZ, 136, HALF)] * 2, [acc, edge, own, other]
    mine, theirs = on_blocks(arrange_kernel, halves, scalars, [], vectors, flops=0)
    parts = exchange(mine + swap(theirs))

    image, sums = local(image_kernel, [shape(64, BLK), shape(16, 8, 128)], parts, slab, weights)
    sums = lax.all_to_all(sums, "sec", 0, 0)
    outs = [shape(64, BLK), shape(8, BLK), shape(NZ, 136, HALF)]
    scaled, norm, sent = local(scaled_kernel, outs, sums, image, slab, weights)

    own = exchange(sent)
    other = swap(own)
    strip = shape(NZ, ROWS, BLK)
    outs = [ACC, strip, strip, shape(2, NZ, ROWS, BLK), shape(8, HALF)]
    acc, low, high, given, totals = on_blocks(last_edge_kernel, outs, scalars, [], [*edge_parts, own, other])
    given = swap(given)
    from_high = lax.ppermute(low + given[0], "sec", DOWN)
    from_low = lax.ppermute(high + given[1], "sec", UP)
    outs, vectors = [ACC, *[shape(NZ, 64, BLK)] * 2], [*inner_parts, own, other, acc]
    _, mine, theirs = on_blocks(last_inner_kernel, outs, scalars, [], vectors, alias={5: 0})
    vectors = [mine, swap(theirs), from_low, from_high]
    (sent,) = on_blocks(last_sums_kernel, [shape(NZ, 64, BLK)], scalars, [], vectors, flops=0)
    parts = exchange(sent)
    finish = functools.partial(finish_kernel, float(entries))
    correction, image_new = local(finish, [shape(64, BLK)] * 2, parts, image, slab, scaled, norm, totals)
    return correction.reshape(wavefunction.shape), image_new.reshape(wavefunction.shape)


def solution(mesh):
    placed = (
        P("sec", "ops", None),
        P("ops", "sec", None, None),
        P("ops", "sec", None, None),
        P("sec", "ops", None),
        P("ops"),
        P("ops", "sec"),
    )
    return jax.shard_map(
        on_device,
        mesh=mesh,
        in_specs=placed,
        out_specs=(P("sec", "ops", None), P("sec", "ops", None)),
        check_vma=False,
    )
```
